256 devices in a mesh: row: 16 (over x, z_lo, core), col: 16 (over y, z_hi).
Axes of the slice: x: 4, y: 4, z: 8 (z_hi: 4, z_lo: 2; z = z_hi * 2 + z_lo), core: 2. Of those that a mesh axis runs over, the one named last changes fastest.
Arguments:
- panel_prev: float32 [64, 262144], P(None, 'col'), may hold values from -6 to 6
- panel_cur: float32 [64, 262144], P(None, 'col'), may hold values from -6 to 6
- tiles: float32 [16, 16, 163, 128, 128], P('row', 'col'), may hold values from -0.25 to 0.25
- tile_rows: int32 [16, 16, 163], P('row', 'col'), may hold values from 0 to 127, as said below
- tile_cols: int32 [16, 16, 163], P('row', 'col'), may hold values from 0 to 127, as said below
- tile_count: int32 [16, 16], P('row', 'col'), may hold values from 1 to 163, as said below
- center: float32 [], replicated, may hold values from -0.3 to 0.3
- halfwidth: float32 [], replicated, may hold values from 0.8 to 1.6
Outputs:
- panel_next: float32 [64, 262144], P(None, 'col')
- panel_last: float32 [64, 262144], P(None, 'col')
The draws below stay inside these ranges and needn't reach their ends.
Inputs may be any that keep to these rules, and one draw needn't show every extreme that they name: `tile_rows`: in each grid cell the first tile_count slots name distinct block pairs; later slots hold 0. `tile_cols`: paired with tile_rows slot by slot; later slots hold 0. `tile_count`: some grid cell holds exactly 163 tiles in every draw.
All inputs are finite; a program needn't handle non-finite values.
Results may differ from the reference program's by a relative error of at most 0.0003.
Values sent between devices are 32-bit elements; how exact they have to be, the bound alone decides.
No kernel may reach another device: no remote copies, remote signals or barrier semaphores. Data moves between devices by JAX's collectives and lax.ppermute only.
A program may use at most 128 MiB of HBM per device.

```python
import jax
import jax.numpy as jnp
from jax import lax

B = 128
VEC = 64
BLK_COL = 128
BLOCKS = 2048
ORDER = 262144
SHARE_BLK = 8
TILE_CAP = 163
N_ROW = 16
N_COL = 16


def tile_pattern(key):
    cells = N_ROW * N_COL
    area = BLOCKS // N_ROW * BLK_COL
    cell_keys = jax.random.split(jax.random.fold_in(key, 11), cells)
    picks = jax.vmap(lambda cell_key: jax.random.permutation(cell_key, area)[:TILE_CAP])(cell_keys)
    picks = picks.astype(jnp.int32)
    first = jax.random.randint(jax.random.fold_in(key, 12), (cells,), 0, TILE_CAP)
    second = jax.random.randint(jax.random.fold_in(key, 13), (cells,), 0, TILE_CAP)
    counts = 1 + first * second // TILE_CAP
    busiest = jax.random.randint(jax.random.fold_in(key, 14), (), 0, cells)
    counts = jnp.where(lax.iota(jnp.int32, cells) == busiest, TILE_CAP, counts).astype(jnp.int32)
    live = lax.iota(jnp.int32, TILE_CAP)[None, :] < counts[:, None]
    picks = jnp.where(live, picks, 0)
    rows = (picks // BLK_COL).reshape(N_ROW, N_COL, TILE_CAP).astype(jnp.int32)
    cols = (picks % BLK_COL).reshape(N_ROW, N_COL, TILE_CAP).astype(jnp.int32)
    return (rows, cols, counts.reshape(N_ROW, N_COL))


def draw_tile_rows(key, part):
    return tile_pattern(key)[0]


def draw_tile_cols(key, part):
    return tile_pattern(key)[1]


def draw_tile_count(key, part):
    return tile_pattern(key)[2]


def shard_levels(stream_key, shape, cuts, low, high):
    gain = 1.0
    for axis_at, shards_of in cuts:
        steps = jax.random.uniform(jax.random.fold_in(jax.random.fold_in(stream_key, 6), axis_at), (shards_of,), jnp.float32, low / len(cuts), high / len(cuts))
        gain = gain * jnp.repeat(jnp.exp(steps), shape[axis_at] // shards_of).reshape((-1,) + (1,) * (len(shape) - 1 - axis_at))
    return gain


def scatter_about(stream_key, extent, width, bound, cuts=(), held_as=jnp.bfloat16):
    factor_of = shard_levels(stream_key, extent, cuts, -0.22, 0.18) if cuts else 1.0
    array = jax.random.normal(stream_key, extent, jnp.float32) * width * factor_of
    return jnp.minimum(jnp.maximum(array, -bound), bound).astype(held_as)


def setup_inputs(seed: int = 0) -> dict:
    key_of = jax.random.split(jax.random.key(seed), 9)
    panel_prev = scatter_about(key_of[0], (VEC, ORDER), 1.0, 6.0, ((1, 16),), jnp.float32)
    panel_cur = scatter_about(key_of[1], (VEC, ORDER), 1.0, 6.0, ((1, 16),), jnp.float32)
    tiles = scatter_about(key_of[2], (N_ROW, N_COL, TILE_CAP, B, B), (4 * B) ** -0.5, 0.25, ((0, 16), (1, 16)), jnp.float32)
    tile_rows = draw_tile_rows(jax.random.fold_in(key_of[8], 71), 0)
    tile_cols = draw_tile_cols(jax.random.fold_in(key_of[8], 71), 0)
    tile_count = draw_tile_count(jax.random.fold_in(key_of[8], 71), 0)
    center = jnp.clip(jax.random.uniform(key_of[6], (), jnp.float32, -0.3, 0.3), -0.3, 0.3)
    halfwidth = jnp.clip(jax.random.uniform(key_of[7], (), jnp.float32, 0.8, 1.6), 0.8, 1.6)
    return dict(panel_prev=panel_prev, panel_cur=panel_cur, tiles=tiles, tile_rows=tile_rows, tile_cols=tile_cols, tile_count=tile_count, center=center, halfwidth=halfwidth)


def device_product(piece, tile_block, rows, cols, count):
    vectors = piece.shape[0]
    row_blocks = BLOCKS // N_ROW
    blocked = piece.reshape(vectors, BLK_COL, B)
    chosen = jnp.take(blocked, cols, axis=1)
    products = jnp.einsum("vtk,tjk->tvj", chosen, tile_block, precision=lax.Precision.HIGHEST)
    live = (lax.iota(jnp.int32, TILE_CAP) < count).astype(jnp.float32)
    onehot = (rows[:, None] == lax.iota(jnp.int32, row_blocks)[None, :]).astype(jnp.float32) * live[:, None]
    summed = jnp.einsum("tr,tvj->vrj", onehot, products, precision=lax.Precision.HIGHEST)
    return summed.reshape(vectors, row_blocks * B)


def apply_operator(panel, tiles, tile_rows, tile_cols, tile_count):
    vectors = panel.shape[0]
    pieces = panel.reshape(vectors, N_COL, BLK_COL * B)

    def one_row(row_index):
        def add_cell(total, col_index):
            piece = lax.dynamic_index_in_dim(pieces, col_index, 1, keepdims=False)
            term = device_product(piece, tiles[row_index, col_index], tile_rows[row_index, col_index],
                                  tile_cols[row_index, col_index], tile_count[row_index, col_index])
            return total + term, None
        start = jnp.zeros((vectors, (BLOCKS // N_ROW) * B), jnp.float32)
        return lax.scan(add_cell, start, jnp.arange(N_COL, dtype=jnp.int32))[0]

    by_rows = lax.map(one_row, jnp.arange(N_ROW, dtype=jnp.int32))
    by_rows = by_rows.reshape(N_ROW, vectors, N_COL, SHARE_BLK * B)
    return jnp.transpose(by_rows, (1, 2, 0, 3)).reshape(vectors, ORDER)


def reference(panel_prev, panel_cur, tiles, tile_rows, tile_cols, tile_count, center, halfwidth):
    factor = 2.0 / halfwidth
    image_one = apply_operator(panel_cur, tiles, tile_rows, tile_cols, tile_count)
    panel_next = factor * (image_one - center * panel_cur) - panel_prev
    image_two = apply_operator(panel_next, tiles, tile_rows, tile_cols, tile_count)
    panel_last = factor * (image_two - center * panel_next) - panel_cur
    return panel_next, panel_last
```

```python
import functools

import jax
import jax.numpy as jnp
from jax import lax
from jax.experimental import pallas as pl
from jax.experimental.pallas import tpu as pltpu
from jax.sharding import Mesh, PartitionSpec as P

B = 128
BLK = 128
CAP = 163
CHUNK = 8
GROUPS = 2
VEC = 64
V = VEC // GROUPS
ROW = ("x", "zl", "core")
COL = ("y", "zh")


def split(value):
    high = value.astype(jnp.bfloat16)
    return high, (value - high.astype(jnp.float32)).astype(jnp.bfloat16)


def product_kernel(flat, rows, cols, info, x_ref, tiles, own, plus, minus, far, xs, acc, held, sems):
    count, mine = info[0], info[1]
    chunks = -(-CAP // CHUNK)
    for c in range(chunks):
        size = min(CHUNK, CAP - c * CHUNK)

        @pl.when(c * CHUNK < count)
        def _():
            span = pl.ds(c * CHUNK, size)
            pltpu.make_async_copy(tiles.at[span], held.at[span], sems.at[c]).start()

    for c in range(BLK):
        block = x_ref[:, c * B : (c + 1) * B] if flat else x_ref[c]
        high, low = split(block)
        xs[c, :V] = high
        xs[c, V:] = low
    acc[...] = jnp.zeros_like(acc)

    def some(first, size):
        sums = []
        for u in range(size):
            slot = first + u
            high, low = split(held[slot])
            both = jnp.concatenate([high, low], axis=0)
            p = lax.dot_general(
                xs[cols[slot]], both, (((1,), (1,)), ((), ())), preferred_element_type=jnp.float32
            )
            sums.append(p[:V, :B] + (p[V:, :B] + p[:V, B:]))
        for u in range(size):
            slot = first + u
            at = jnp.where(slot < count, lax.rem(rows[slot] + (4 - mine) * 32, BLK), BLK)
            acc[at] += sums[u]

    whole = CAP // CHUNK

    def step(c, carry):
        span = pl.ds(c * CHUNK, CHUNK)
        pltpu.make_async_copy(tiles.at[span], held.at[span], sems.at[c]).wait()
        some(c * CHUNK, CHUNK)
        return carry

    lax.fori_loop(0, jnp.minimum((count + CHUNK - 1) // CHUNK, whole), step, 0)

    if CAP % CHUNK:

        @pl.when(count > whole * CHUNK)
        def _():
            span = pl.ds(whole * CHUNK, CAP % CHUNK)
            pltpu.make_async_copy(tiles.at[span], held.at[span], sems.at[whole]).wait()
            some(whole * CHUNK, CAP % CHUNK)

    own[...] = acc[0:32]
    plus[...] = acc[32:64]
    far[...] = acc[64:96]
    minus[...] = acc[96:128]


def product(x, tiles, rows, cols, info, group):
    flat = x.ndim == 2
    x_spec = (
        pl.BlockSpec((V, BLK * B), lambda _: (group, 0))
        if flat
        else pl.BlockSpec((BLK, V, B), lambda _: (0, 0, 0))
    )
    smem = pl.BlockSpec(memory_space=pltpu.SMEM)
    piece = pl.BlockSpec((32, V, B), lambda _: (0, 0, 0))
    return pl.pallas_call(
        functools.partial(product_kernel, flat),
        grid=(1,),
        out_shape=[jax.ShapeDtypeStruct((32, V, B), jnp.float32)] * 4,
        in_specs=[smem, smem, smem, x_spec, pl.BlockSpec(memory_space=pl.ANY)],
        out_specs=[piece] * 4,
        scratch_shapes=[
            pltpu.VMEM((BLK, 2 * V, B), jnp.bfloat16),
            pltpu.VMEM((BLK + 1, V, B), jnp.float32),
            pltpu.VMEM((CAP, B, B), jnp.float32),
            pltpu.SemaphoreType.DMA((-(-CAP // CHUNK),)),
        ],
        compiler_params=pltpu.CompilerParams(vmem_limit_bytes=40 << 20),
        cost_estimate=pl.CostEstimate(
            flops=CAP * B * B * VEC * 8, bytes_accessed=CAP * B * B * 4, transcendentals=0
        ),
        name="product",
    )(rows, cols, info, x, tiles)


def add_kernel(info, a, b, c, d, own, plus, minus, far):
    mine = info[2]
    for k, out in enumerate((own, plus, far, minus)):
        span = pl.ds(lax.rem(mine + k, 4) * 8, 8)
        out[...] = (a[span] + b[span]) + (c[span] + d[span])


def add_pieces(info, parts):
    smem = pl.BlockSpec(memory_space=pltpu.SMEM)
    return pl.pallas_call(
        add_kernel,
        out_shape=[jax.ShapeDtypeStruct((8, V, B), jnp.float32)] * 4,
        in_specs=[smem] + [pl.BlockSpec(memory_space=pltpu.VMEM)] * 4,
        out_specs=[pl.BlockSpec(memory_space=pltpu.VMEM)] * 4,
        name="add_pieces",
    )(info, *parts)


def combine_kernel(scal, a, b, c, d, cur, prev, out):
    factor, center = scal[0], scal[1]
    image = (a[...] + b[...]) + (c[...] + d[...])
    out[...] = factor * (image - center * cur[...]) - prev[...]


def combine(scal, parts, cur, prev):
    smem = pl.BlockSpec(memory_space=pltpu.SMEM)
    vmem = pl.BlockSpec(memory_space=pltpu.VMEM)
    return pl.pallas_call(
        combine_kernel,
        out_shape=jax.ShapeDtypeStruct((8, V, B), jnp.float32),
        in_specs=[smem] + [vmem] * 6,
        out_specs=vmem,
        name="combine",
    )(scal, *parts, cur, prev)


def spread(parts, axis):
    own, plus, minus, far = parts
    return (
        own,
        lax.ppermute(plus, axis, [(i, (i + 1) % 4) for i in range(4)]),
        lax.ppermute(minus, axis, [(i, (i + 3) % 4) for i in range(4)]),
        lax.ppermute(far, axis, [(i, (i + 2) % 4) for i in range(4)]),
    )


def own_share(panel, row):
    mine = lax.dynamic_slice_in_dim(panel, row * 8 * B, 8 * B, 1)
    blocked = jnp.transpose(mine.reshape(GROUPS, V, 8, B), (0, 2, 1, 3))
    return [blocked[g] for g in range(GROUPS)]


def body(panel_prev, panel_cur, tiles, tile_rows, tile_cols, tile_count, center, halfwidth):
    tiles = tiles.reshape(CAP, B, B)
    rows = tile_rows.reshape(CAP)
    cols = tile_cols.reshape(CAP)
    info = jnp.stack([tile_count.reshape(()), lax.axis_index("y"), lax.axis_index("zh")]).astype(jnp.int32)
    scal = jnp.stack([2.0 / halfwidth, center])
    row = lax.axis_index(ROW)
    cur = own_share(panel_cur, row)
    prev = own_share(panel_prev, row)

    def degree(x, group, cur, prev):
        parts = product(x, tiles, rows, cols, info, group)
        parts = add_pieces(info, spread(parts, "y"))
        share = combine(scal, spread(parts, "zh"), cur, prev)
        whole = lax.all_gather(share, ROW).reshape(BLK, V, B)
        return share, whole

    nexts = [degree(panel_cur, g, cur[g], prev[g]) for g in range(GROUPS)]
    lasts = [degree(nexts[g][1], g, nexts[g][0], cur[g]) for g in range(GROUPS)]

    def panel(wholes):
        return jnp.concatenate([jnp.transpose(w, (1, 0, 2)).reshape(V, BLK * B) for _, w in wholes])

    return panel(nexts), panel(lasts)


def solution(mesh):
    fine = Mesh(mesh.devices.reshape(4, 2, 2, 4, 4), ROW + COL)
    placed = (
        P(None, COL),
        P(None, COL),
        P(ROW, COL, None, None, None),
        P(ROW, COL, None),
        P(ROW, COL, None),
        P(ROW, COL),
        P(),
        P(),
    )
    return jax.shard_map(
        body, mesh=fine, in_specs=placed, out_specs=(P(None, COL), P(None, COL)), check_vma=False
    )
```

```python
import functools

import jax
import jax.numpy as jnp
from jax import lax
from jax.experimental import pallas as pl
from jax.experimental.pallas import tpu as pltpu
from jax.sharding import Mesh, PartitionSpec as P

B = 128
BLK = 128
CAP = 163
CHUNK = 16
VEC = 64
SIZES = (16, 24, 24)
FIRST = tuple(sum(SIZES[:g]) for g in range(len(SIZES)))
ROW = ("x", "zl", "core")
COL = ("y", "zh")
ORDER = (
    "A0s", "B0s", "A0a", "C0s", "A0b", "B0a", "C0a", "A0c", "B0b", "C0b", "A0d", "B0c", "A0e",
    "C0c", "A0f", "B0d", "C0d", "A0g", "B0e", "C0e", "A1p", "C0f", "B0f", "A1a", "C0g", "B0g",
    "C1p", "A1b", "B1p", "A1c", "C1a", "A1d", "B1a", "C1b", "A1e", "B1b", "A1f", "C1c", "B1c",
    "C1d", "B1d", "C1e", "B1e", "C1f", "B1f", "A1g", "C1g", "A1m", "B1g", "C1m", "B1m",
)


def split(value):
    high = value.astype(jnp.bfloat16).astype(jnp.float32)
    return jnp.concatenate([high, value - high], axis=0).astype(jnp.bfloat16)


def ring_place(rel, core):
    one, three = 2 - core, 1 + core
    return jnp.where(rel == 0, 0, jnp.where(rel == 2, 3, jnp.where(rel == 1, one, three)))


def row_places(table):
    core, y, zh = (lax.axis_index(a) for a in ("core", "y", "zh"))
    for q in range(16):
        table[q] = ring_place(q // 4 ^ y, core) * 32 + ring_place(q % 4 ^ zh, core) * 8


def col_places(table, owners):
    x, zl, core = (lax.axis_index(a) for a in ROW)
    for r in range(16):
        side = r % 2
        spot = (side ^ core) * 8 + ring_place(r // 4 ^ x, 1 - side) * 2 + (r // 2 % 2 ^ zl)
        table[r] = spot * 8
        owners[spot] = r


def read_pattern(pattern, held, sems):
    copies = [pltpu.make_async_copy(p, h, sems.at[k]) for k, (p, h) in enumerate(zip(pattern, held))]
    for copy in copies:
        copy.start()
    return copies


def copy_tiles(tiles, held, sems):
    def one(c, size):
        span = pl.ds(c * CHUNK, size)
        return pltpu.make_async_copy(tiles.at[0, 0, span], held.at[span], sems.at[c])

    return one


def multiply(start, size, count, rows, cols, row_table, col_table, xs, held, acc):
    v = acc.shape[1]
    sums = []
    for u in range(size):
        col = cols[0, 0, start + u]
        if col_table is not None:
            col = col_table[col // 8] + col % 8
        p = lax.dot_general(
            xs[col], split(held[start + u]), (((1,), (1,)), ((), ())), preferred_element_type=jnp.float32
        )
        sums.append(p[:v, :B] + (p[v:, :B] + p[:v, B:]))
    for u in range(size):
        row = rows[0, 0, start + u]
        acc[jnp.where(start + u < count, row_table[row // 8] + row % 8, BLK)] += sums[u]


def over_chunks(count, work):
    whole = CAP // CHUNK

    def step(c, carry):
        work(c, CHUNK)
        return carry

    lax.fori_loop(0, jnp.minimum((count + CHUNK - 1) // CHUNK, whole), step, 0)
    if CAP % CHUNK:

        @pl.when(count > whole * CHUNK)
        def _():
            work(whole, CAP % CHUNK)


def send_out(acc, parts, outs, sems):
    copies = []
    for k, out in enumerate(outs):
        place = acc.at[pl.ds(k % 2 * 64, 64), pl.ds(sum(parts[: k // 2]), parts[k // 2])]
        copies.append(pltpu.make_async_copy(place, out, sems.at[k]))
    for copy in copies:
        copy.start()
    for copy in copies:
        copy.wait()


PATTERN = [pltpu.SMEM((1, 1, CAP), jnp.int32)] * 2
TABLES = [pltpu.SMEM((16,), jnp.int32)] * 3
TILES = [
    pltpu.VMEM((CAP, B, B), jnp.float32),
    pltpu.SemaphoreType.DMA((-(-CAP // CHUNK),)),
    pltpu.SemaphoreType.DMA((2,)),
]


def start_tiles(count, tile_copy):
    for c in range(-(-CAP // CHUNK)):

        @pl.when(c * CHUNK < count)
        def _():
            tile_copy(c, min(CHUNK, CAP - c * CHUNK)).start()


def first_kernel(live, rows_in, cols_in, tiles, panel_cur, panel_prev, *refs):
    n = 2 * len(SIZES)
    outs, (cur, prev), refs = refs[:n], refs[n : n + 2], refs[n + 2 :]
    (rows, cols), (row_table, _, _), (held, sems, p_sems) = refs[:2], refs[2:5], refs[5:8]
    xf, xp, xs, acc, x_sems, out_sems = refs[8:]
    mine = pl.multiple_of(((lax.axis_index("x") * 2 + lax.axis_index("zl")) * 2 + lax.axis_index("core")) * (8 * B), 8 * B)
    pattern = read_pattern((rows_in, cols_in), (rows, cols), p_sems)
    x_copy = pltpu.make_async_copy(panel_cur, xf, x_sems.at[0])
    p_copy = pltpu.make_async_copy(panel_prev.at[:, pl.ds(mine, 8 * B)], xp, x_sems.at[1])
    x_copy.start()
    count = live[0, 0]
    tile_copy = copy_tiles(tiles, held, sems)
    start_tiles(count, tile_copy)
    p_copy.start()
    row_places(row_table)
    acc[...] = jnp.zeros_like(acc)
    x_copy.wait()
    for c in range(BLK):
        xs[c] = split(xf[:, c * B : (c + 1) * B])
    for copy in pattern:
        copy.wait()
    for b in range(8):
        cur[b] = xf[:, pl.ds(mine + b * B, B)]

    def work(c, size):
        tile_copy(c, size).wait()
        multiply(c * CHUNK, size, count, rows, cols, row_table, None, xs, held, acc)

    over_chunks(count, work)
    p_copy.wait()
    for b in range(8):
        prev[b] = xp[:, b * B : (b + 1) * B]
    send_out(acc, SIZES, outs, out_sems)


def first_products(count, pattern, tiles, panel_cur, panel_prev):
    hbm = [pltpu.with_memory_space_constraint(a, pltpu.HBM) for a in (*pattern, tiles, panel_cur, panel_prev)]
    free = pl.BlockSpec(memory_space=pl.ANY)
    vmem = pl.BlockSpec(memory_space=pltpu.VMEM)
    n = 2 * len(SIZES)
    outs = pl.pallas_call(
        first_kernel,
        out_shape=[pltpu.VMEM((64, v, B), jnp.float32) for v in SIZES for _ in range(2)]
        + [pltpu.VMEM((8, VEC, B), jnp.float32)] * 2,
        in_specs=[pl.BlockSpec(memory_space=pltpu.SMEM)] + [free] * 5,
        out_specs=[free] * n + [vmem] * 2,
        scratch_shapes=PATTERN + TABLES + TILES + [
            pltpu.VMEM((VEC, BLK * B), jnp.float32),
            pltpu.VMEM((VEC, 8 * B), jnp.float32),
            pltpu.VMEM((BLK, 2 * VEC, B), jnp.bfloat16),
            pltpu.VMEM((BLK + 1, VEC, B), jnp.float32),
            pltpu.SemaphoreType.DMA((2,)),
            pltpu.SemaphoreType.DMA((n,)),
        ],
        compiler_params=pltpu.CompilerParams(vmem_limit_bytes=26 << 20),
        cost_estimate=pl.CostEstimate(flops=1, bytes_accessed=1, transcendentals=0),
        name="first",
    )(count, *hbm)
    return [outs[i : i + 2] for i in range(0, n, 2)], outs[n], outs[n + 1]


def lay_out(x_own, x_other, owners, flat):
    for k in range(BLK // 8):
        start = pl.multiple_of(owners[k] * (8 * B), 8 * B)
        ref = x_own if k < 8 else x_other
        for b in range(8):
            flat[:, pl.ds(start + b * B, B)] = ref[k % 8 * 8 + b]


def second_kernel(first, live, rows_in, cols_in, tiles, x_own, x_other, *refs):
    keep, send, panel = refs[-16:-13]
    refs = refs[-13:]
    (rows, cols), (row_table, col_table, owners), (held, sems, p_sems) = refs[:2], refs[2:5], refs[5:8]
    xs, acc, flat, sem, out_sems = refs[8:]
    v = acc.shape[1]
    pattern = read_pattern((rows_in, cols_in), (rows, cols), p_sems)
    count = live[0, 0]
    tile_copy = copy_tiles(tiles, held, sems)
    start_tiles(count, tile_copy)
    row_places(row_table)
    col_places(col_table, owners)
    lay_out(x_own, x_other, owners, flat)
    rows_copy = pltpu.make_async_copy(flat, panel.at[pl.ds(first, v)], sem)
    rows_copy.start()
    acc[...] = jnp.zeros_like(acc)
    for c in range(BLK):
        xs[c] = split((x_own if c < 64 else x_other)[c % 64])
    for copy in pattern:
        copy.wait()

    def work(c, size):
        tile_copy(c, size).wait()
        multiply(c * CHUNK, size, count, rows, cols, row_table, col_table, xs, held, acc)

    over_chunks(count, work)
    send_out(acc, (v,), (keep, send), out_sems)
    rows_copy.wait()


def second_products(count, pattern, tiles, x, panel, g):
    v = SIZES[g]
    free = pl.BlockSpec(memory_space=pl.ANY)
    vmem = pl.BlockSpec(memory_space=pltpu.VMEM)
    hbm = [pltpu.with_memory_space_constraint(a, pltpu.HBM) for a in (*pattern, tiles)]
    near = [pltpu.with_memory_space_constraint(a, pltpu.VMEM) for a in x]
    old = [] if panel is None else [panel]
    return pl.pallas_call(
        functools.partial(second_kernel, FIRST[g]),
        out_shape=[pltpu.VMEM((64, v, B), jnp.float32)] * 2 + [pltpu.HBM((VEC, BLK * B), jnp.float32)],
        in_specs=[pl.BlockSpec(memory_space=pltpu.SMEM)] + [free] * 3 + [vmem] * 2 + [free] * len(old),
        out_specs=[free] * 3,
        scratch_shapes=PATTERN + TABLES + TILES + [
            pltpu.VMEM((BLK, 2 * v, B), jnp.bfloat16),
            pltpu.VMEM((BLK + 1, v, B), jnp.float32),
            pltpu.VMEM((v, BLK * B), jnp.float32),
            pltpu.SemaphoreType.DMA,
            pltpu.SemaphoreType.DMA((2,)),
        ],
        input_output_aliases={6: 2} if old else {},
        compiler_params=pltpu.CompilerParams(vmem_limit_bytes=20 << 20),
        cost_estimate=pl.CostEstimate(flops=1, bytes_accessed=1, transcendentals=0),
        name="second",
    )(count, *hbm, *near, *old)


def assemble_kernel(first, v, x_own, x_other, *rest):
    out, table, owners, flat, sem = rest[-5:]
    col_places(table, owners)
    lay_out(x_own, x_other, owners, flat)
    copy = pltpu.make_async_copy(flat, out.at[pl.ds(first, v)], sem)
    copy.start()
    copy.wait()


def assemble(x, panel, g):
    v = SIZES[g]
    free = pl.BlockSpec(memory_space=pl.ANY)
    vmem = pl.BlockSpec(memory_space=pltpu.VMEM)
    held = [pltpu.with_memory_space_constraint(a, pltpu.VMEM) for a in x]
    old = [] if panel is None else [panel]
    return pl.pallas_call(
        functools.partial(assemble_kernel, FIRST[g], v),
        out_shape=pltpu.HBM((VEC, BLK * B), jnp.float32),
        in_specs=[vmem, vmem] + [free] * len(old),
        out_specs=free,
        scratch_shapes=TABLES[:2] + [pltpu.VMEM((v, BLK * B), jnp.float32), pltpu.SemaphoreType.DMA],
        input_output_aliases={2: 0} if old else {},
        compiler_params=pltpu.CompilerParams(vmem_limit_bytes=8 << 20),
        cost_estimate=pl.CostEstimate(flops=1, bytes_accessed=1, transcendentals=0),
        name="assemble",
    )(*held, *old)


def swap(value, axis):
    return lax.ppermute(value, axis, [(0, 1), (1, 0)])


def exchange(value, axis, turn):
    flip = {(0, 0): 1, (0, 1): 3, (1, 0): 3, (1, 1): 1}
    both, at = (("x", "core"), lambda c, i: i * 2 + c) if axis == "x" else (("core", axis), lambda c, i: c * 4 + i)
    pairs = [(at(c, i), at(c, i ^ flip[c, turn])) for c in range(2) for i in range(4)]
    return lax.ppermute(value, both, pairs)


def body(panel_prev, panel_cur, tiles, tile_rows, tile_cols, tile_count, center, halfwidth):
    pattern = (tile_rows, tile_cols)
    factor = 2.0 / halfwidth
    shares = {}
    panels = [None, None]

    first, cur, prev = first_products(tile_count, pattern, tiles, panel_cur, panel_prev)
    token = first[0][0]
    state = {(g, 0): [[keep], send] for g, (keep, send) in enumerate(first)}

    for event in ORDER:
        g, step, stage = ord(event[0]) - 65, int(event[1]), event[2]
        key = (g, step)
        if stage == "s":
            (state[key][1],), token = lax.optimization_barrier(((state[key][1],), token))
            continue
        if stage == "p":
            args, token = lax.optimization_barrier((state[g, 0], token))
            keep, token, panels[0] = second_products(tile_count, pattern, tiles, args, panels[0], g)
            state[key] = [[keep], token]
            continue
        if stage == "m":
            args, token = lax.optimization_barrier((state[key], token))
            panels[1] = token = assemble(args, panels[1], g)
            continue
        if stage in "abcd":
            kept, send = state[key]
            got = exchange(send, "y" if stage in "ab" else "zh", "abcd".index(stage) % 2)
        elif stage == "e":
            kept, got = [state[key]], swap(state[key], "zl")
        else:
            kept, got = [state[key]], exchange(state[key], "x", "fg".index(stage))
        (kept, got), token = lax.optimization_barrier(((kept, got), token))
        kept = [*kept, got]
        if stage in "abc":
            half = got.shape[0] // 2
            token = functools.reduce(jnp.add, [piece[half : 2 * half] for piece in kept])
            state[key] = [kept, token]
        elif stage == "d":
            mine = slice(FIRST[g], FIRST[g] + SIZES[g])
            now, before = (cur[:, mine], prev[:, mine]) if step == 0 else (shares[g], cur[:, mine])
            image = functools.reduce(jnp.add, [piece[: got.shape[0]] for piece in kept])
            state[key] = shares[g] = token = factor * (image - center * now) - before
        else:
            state[key] = token = jnp.concatenate(kept)
            if stage == "g":
                state[key] = [state[key], swap(state[key], "core")]
    return tuple(panels)


def solution(mesh):
    fine = Mesh(mesh.devices.reshape(4, 2, 2, 4, 4), ROW + COL)
    placed = (
        P(None, COL),
        P(None, COL),
        P(ROW, COL, None, None, None),
        P(ROW, COL, None),
        P(ROW, COL, None),
        P(ROW, COL),
        P(),
        P(),
    )
    return jax.shard_map(
        body, mesh=fine, in_specs=placed, out_specs=(P(None, COL), P(None, COL)), check_vma=False
    )
```

```python
import functools

import jax
import jax.numpy as jnp
from jax import lax
from jax.experimental import pallas as pl
from jax.experimental.pallas import tpu as pltpu
from jax.sharding import Mesh, PartitionSpec as P

B = 128
BLK = 128
CAP = 163
CHUNKS = (32, 16)
VEC = 64
SIZES = (16, 24, 24)
FIRST = tuple(sum(SIZES[:g]) for g in range(len(SIZES)))
ROW = ("x", "zl", "core")
COL = ("y", "zh")
ORDER = (
    "A0s", "B0s", "C0s", "A0a", "A0b", "B0a", "C0a", "A0c", "B0b", "C0b", "A0d", "B0c", "A0e",
    "C0c", "A0f", "B0d", "C0d", "B0e", "A0g", "C0e", "B0f", "C0f", "A1p", "B0g", "C0g", "B1p",
    "A1a", "C1p", "A1b", "B1a", "A1c", "C1a", "B1b", "A1d", "C1b", "B1c", "A1e", "C1c", "A1f",
    "B1d", "C1d", "B1e", "A1g", "C1e", "B1f", "C1f", "A1m", "B1g", "C1g", "B1m", "C1m",
)


def split(value):
    high = value.astype(jnp.bfloat16).astype(jnp.float32)
    return jnp.concatenate([high, value - high], axis=0).astype(jnp.bfloat16)


def ring_place(rel, core):
    one, three = 2 - core, 1 + core
    return jnp.where(rel == 0, 0, jnp.where(rel == 2, 3, jnp.where(rel == 1, one, three)))


def row_places(table):
    core, y, zh = (lax.axis_index(a) for a in ("core", "y", "zh"))
    for q in range(16):
        table[q] = ring_place(q // 4 ^ y, core) * 32 + ring_place(q % 4 ^ zh, core) * 8


def col_places(table, owners):
    x, zl, core = (lax.axis_index(a) for a in ROW)
    for r in range(16):
        side = r % 2
        spot = (side ^ core) * 8 + ring_place(r // 4 ^ x, 1 - side) * 2 + (r // 2 % 2 ^ zl)
        table[r] = spot * 8
        owners[spot] = r


def read_pattern(pattern, held, sems):
    copies = [pltpu.make_async_copy(p, h, sems.at[k]) for k, (p, h) in enumerate(zip(pattern, held))]
    for copy in copies:
        copy.start()
    return copies


def copy_tiles(tiles, held, sems, chunk):
    def one(c, size):
        span = pl.ds(c * chunk, size)
        return pltpu.make_async_copy(tiles.at[0, 0, span], held.at[span], sems.at[c])

    return one


def multiply(start, size, count, rows, cols, row_table, col_table, xs, held, acc):
    v = acc.shape[1]
    sums = []
    for u in range(size):
        col = cols[0, 0, start + u]
        if col_table is not None:
            col = col_table[col // 8] + col % 8
        p = lax.dot_general(
            xs[col], split(held[start + u]), (((1,), (1,)), ((), ())), preferred_element_type=jnp.float32
        )
        sums.append(p[:v, :B] + (p[v:, :B] + p[:v, B:]))
    for u in range(size):
        row = rows[0, 0, start + u]
        acc[jnp.where(start + u < count, row_table[row // 8] + row % 8, BLK)] += sums[u]


def over_chunks(count, chunk, work):
    whole = CAP // chunk

    def step(c, carry):
        work(c, chunk)
        return carry

    lax.fori_loop(0, jnp.minimum((count + chunk - 1) // chunk, whole), step, 0)
    if CAP % chunk:

        @pl.when(count > whole * chunk)
        def _():
            work(whole, CAP % chunk)


def send_out(acc, parts, outs, sems):
    copies = []
    for k, out in enumerate(outs):
        place = acc.at[pl.ds(k % 2 * 64, 64), pl.ds(sum(parts[: k // 2]), parts[k // 2])]
        copies.append(pltpu.make_async_copy(place, out, sems.at[k]))
    for copy in copies:
        copy.start()
    for copy in copies:
        copy.wait()


PATTERN = [pltpu.SMEM((1, 1, CAP), jnp.int32)] * 2
TABLES = [pltpu.SMEM((16,), jnp.int32)] * 3
TILES = [
    pltpu.VMEM((CAP, B, B), jnp.float32),
    pltpu.SemaphoreType.DMA((-(-CAP // min(CHUNKS)),)),
    pltpu.SemaphoreType.DMA((2,)),
]


def start_tiles(count, chunk, tile_copy):
    for c in range(-(-CAP // chunk)):

        @pl.when(c * chunk < count)
        def _():
            tile_copy(c, min(chunk, CAP - c * chunk)).start()


def first_kernel(live, rows_in, cols_in, tiles, panel_cur, panel_prev, *refs):
    n = 2 * len(SIZES)
    outs, (cur, prev), refs = refs[:n], refs[n : n + 2], refs[n + 2 :]
    (rows, cols), (row_table, _, _), (held, sems, p_sems) = refs[:2], refs[2:5], refs[5:8]
    xf, xp, xs, acc, x_sems, out_sems = refs[8:]
    mine = pl.multiple_of(((lax.axis_index("x") * 2 + lax.axis_index("zl")) * 2 + lax.axis_index("core")) * (8 * B), 8 * B)
    pattern = read_pattern((rows_in, cols_in), (rows, cols), p_sems)
    x_copies = []
    for k in range(4):
        span = pl.ds(k * 32 * B, 32 * B)
        x_copies.append(pltpu.make_async_copy(panel_cur.at[:, span], xf.at[:, span], x_sems.at[k]))
        x_copies[k].start()
    p_copy = pltpu.make_async_copy(panel_prev.at[:, pl.ds(mine, 8 * B)], xp, x_sems.at[4])
    count, chunk = live[0, 0], CHUNKS[0]
    tile_copy = copy_tiles(tiles, held, sems, chunk)
    start_tiles(count, chunk, tile_copy)
    p_copy.start()
    row_places(row_table)
    acc[...] = jnp.zeros_like(acc)
    for c in range(BLK):
        if c % 32 == 0:
            x_copies[c // 32].wait()
        xs[c] = split(xf[:, c * B : (c + 1) * B])
    for copy in pattern:
        copy.wait()
    for b in range(8):
        cur[b] = xf[:, pl.ds(mine + b * B, B)]

    def work(c, size):
        tile_copy(c, size).wait()
        multiply(c * chunk, size, count, rows, cols, row_table, None, xs, held, acc)

    over_chunks(count, chunk, work)
    p_copy.wait()
    for b in range(8):
        prev[b] = xp[:, b * B : (b + 1) * B]
    send_out(acc, SIZES, outs, out_sems)


def first_products(count, pattern, tiles, panel_cur, panel_prev):
    hbm = [pltpu.with_memory_space_constraint(a, pltpu.HBM) for a in (*pattern, tiles, panel_cur, panel_prev)]
    free = pl.BlockSpec(memory_space=pl.ANY)
    vmem = pl.BlockSpec(memory_space=pltpu.VMEM)
    n = 2 * len(SIZES)
    outs = pl.pallas_call(
        first_kernel,
        out_shape=[pltpu.VMEM((64, v, B), jnp.float32) for v in SIZES for _ in range(2)]
        + [pltpu.VMEM((8, VEC, B), jnp.float32)] * 2,
        in_specs=[pl.BlockSpec(memory_space=pltpu.SMEM)] + [free] * 5,
        out_specs=[free] * n + [vmem] * 2,
        scratch_shapes=PATTERN + TABLES + TILES + [
            pltpu.VMEM((VEC, BLK * B), jnp.float32),
            pltpu.VMEM((VEC, 8 * B), jnp.float32),
            pltpu.VMEM((BLK, 2 * VEC, B), jnp.bfloat16),
            pltpu.VMEM((BLK + 1, VEC, B), jnp.float32),
            pltpu.SemaphoreType.DMA((5,)),
            pltpu.SemaphoreType.DMA((n,)),
        ],
        compiler_params=pltpu.CompilerParams(vmem_limit_bytes=26 << 20),
        cost_estimate=pl.CostEstimate(flops=1, bytes_accessed=1, transcendentals=0),
        name="first",
    )(count, *hbm)
    return [outs[i : i + 2] for i in range(0, n, 2)], outs[n], outs[n + 1]


def lay_out(x_own, x_other, owners, flat):
    for k in range(BLK // 8):
        start = pl.multiple_of(owners[k] * (8 * B), 8 * B)
        ref = x_own if k < 8 else x_other
        for b in range(8):
            flat[:, pl.ds(start + b * B, B)] = ref[k % 8 * 8 + b]


def second_kernel(first, live, rows_in, cols_in, tiles, x_own, x_other, *refs):
    keep, send, panel = refs[-16:-13]
    refs = refs[-13:]
    (rows, cols), (row_table, col_table, owners), (held, sems, p_sems) = refs[:2], refs[2:5], refs[5:8]
    xs, acc, flat, sem, out_sems = refs[8:]
    v = acc.shape[1]
    pattern = read_pattern((rows_in, cols_in), (rows, cols), p_sems)
    count, chunk = live[0, 0], CHUNKS[1]
    tile_copy = copy_tiles(tiles, held, sems, chunk)
    start_tiles(count, chunk, tile_copy)
    row_places(row_table)
    col_places(col_table, owners)
    lay_out(x_own, x_other, owners, flat)
    rows_copy = pltpu.make_async_copy(flat, panel.at[pl.ds(first, v)], sem)
    rows_copy.start()
    acc[...] = jnp.zeros_like(acc)
    for c in range(BLK):
        xs[c] = split((x_own if c < 64 else x_other)[c % 64])
    for copy in pattern:
        copy.wait()

    def work(c, size):
        tile_copy(c, size).wait()
        multiply(c * chunk, size, count, rows, cols, row_table, col_table, xs, held, acc)

    over_chunks(count, chunk, work)
    send_out(acc, (v,), (keep, send), out_sems)
    rows_copy.wait()


def second_products(count, pattern, tiles, x, panel, g):
    v = SIZES[g]
    free = pl.BlockSpec(memory_space=pl.ANY)
    vmem = pl.BlockSpec(memory_space=pltpu.VMEM)
    hbm = [pltpu.with_memory_space_constraint(a, pltpu.HBM) for a in (*pattern, tiles)]
    near = [pltpu.with_memory_space_constraint(a, pltpu.VMEM) for a in x]
    old = [] if panel is None else [panel]
    return pl.pallas_call(
        functools.partial(second_kernel, FIRST[g]),
        out_shape=[pltpu.VMEM((64, v, B), jnp.float32)] * 2 + [pltpu.HBM((VEC, BLK * B), jnp.float32)],
        in_specs=[pl.BlockSpec(memory_space=pltpu.SMEM)] + [free] * 3 + [vmem] * 2 + [free] * len(old),
        out_specs=[free] * 3,
        scratch_shapes=PATTERN + TABLES + TILES + [
            pltpu.VMEM((BLK, 2 * v, B), jnp.bfloat16),
            pltpu.VMEM((BLK + 1, v, B), jnp.float32),
            pltpu.VMEM((v, BLK * B), jnp.float32),
            pltpu.SemaphoreType.DMA,
            pltpu.SemaphoreType.DMA((2,)),
        ],
        input_output_aliases={6: 2} if old else {},
        compiler_params=pltpu.CompilerParams(vmem_limit_bytes=20 << 20),
        cost_estimate=pl.CostEstimate(flops=1, bytes_accessed=1, transcendentals=0),
        name="second",
    )(count, *hbm, *near, *old)


def assemble_kernel(first, v, x_own, x_other, *rest):
    out, table, owners, flat, sem = rest[-5:]
    col_places(table, owners)
    lay_out(x_own, x_other, owners, flat)
    copy = pltpu.make_async_copy(flat, out.at[pl.ds(first, v)], sem)
    copy.start()
    copy.wait()


def assemble(x, panel, g):
    v = SIZES[g]
    free = pl.BlockSpec(memory_space=pl.ANY)
    vmem = pl.BlockSpec(memory_space=pltpu.VMEM)
    held = [pltpu.with_memory_space_constraint(a, pltpu.VMEM) for a in x]
    old = [] if panel is None else [panel]
    return pl.pallas_call(
        functools.partial(assemble_kernel, FIRST[g], v),
        out_shape=pltpu.HBM((VEC, BLK * B), jnp.float32),
        in_specs=[vmem, vmem] + [free] * len(old),
        out_specs=free,
        scratch_shapes=TABLES[:2] + [pltpu.VMEM((v, BLK * B), jnp.float32), pltpu.SemaphoreType.DMA],
        input_output_aliases={2: 0} if old else {},
        compiler_params=pltpu.CompilerParams(vmem_limit_bytes=8 << 20),
        cost_estimate=pl.CostEstimate(flops=1, bytes_accessed=1, transcendentals=0),
        name="assemble",
    )(*held, *old)


def swap(value, axis):
    return lax.ppermute(value, axis, [(0, 1), (1, 0)])


def exchange(value, axis, turn):
    flip = {(0, 0): 1, (0, 1): 3, (1, 0): 3, (1, 1): 1}
    both, at = (("x", "core"), lambda c, i: i * 2 + c) if axis == "x" else (("core", axis), lambda c, i: c * 4 + i)
    pairs = [(at(c, i), at(c, i ^ flip[c, turn])) for c in range(2) for i in range(4)]
    return lax.ppermute(value, both, pairs)


def body(panel_prev, panel_cur, tiles, tile_rows, tile_cols, tile_count, center, halfwidth):
    pattern = (tile_rows, tile_cols)
    factor = 2.0 / halfwidth
    shares = {}
    panels = [None, None]

    first, cur, prev = first_products(tile_count, pattern, tiles, panel_cur, panel_prev)
    token = first[0][0]
    state = {(g, 0): [[keep], send] for g, (keep, send) in enumerate(first)}

    for event in ORDER:
        g, step, stage = ord(event[0]) - 65, int(event[1]), event[2]
        key = (g, step)
        if stage == "s":
            (state[key][1],), token = lax.optimization_barrier(((state[key][1],), token))
            continue
        if stage == "p":
            args, token = lax.optimization_barrier((state[g, 0], token))
            keep, token, panels[0] = second_products(tile_count, pattern, tiles, args, panels[0], g)
            state[key] = [[keep], token]
            continue
        if stage == "m":
            args, token = lax.optimization_barrier((state[key], token))
            panels[1] = token = assemble(args, panels[1], g)
            continue
        if stage in "abcd":
            kept, send = state[key]
            got = exchange(send, "y" if stage in "ab" else "zh", "abcd".index(stage) % 2)
        elif stage == "e":
            kept, got = [state[key]], swap(state[key], "zl")
        else:
            kept, got = [state[key]], exchange(state[key], "x", "fg".index(stage))
        (kept, got), token = lax.optimization_barrier(((kept, got), token))
        kept = [*kept, got]
        if stage in "abc":
            half = got.shape[0] // 2
            token = functools.reduce(jnp.add, [piece[half : 2 * half] for piece in kept])
            state[key] = [kept, token]
        elif stage == "d":
            mine = slice(FIRST[g], FIRST[g] + SIZES[g])
            now, before = (cur[:, mine], prev[:, mine]) if step == 0 else (shares[g], cur[:, mine])
            image = functools.reduce(jnp.add, [piece[: got.shape[0]] for piece in kept])
            state[key] = shares[g] = token = factor * (image - center * now) - before
        else:
            state[key] = token = jnp.concatenate(kept)
            if stage == "g":
                state[key] = [state[key], swap(state[key], "core")]
    return tuple(panels)


def solution(mesh):
    fine = Mesh(mesh.devices.reshape(4, 2, 2, 4, 4), ROW + COL)
    placed = (
        P(None, COL),
        P(None, COL),
        P(ROW, COL, None, None, None),
        P(ROW, COL, None),
        P(ROW, COL, None),
        P(ROW, COL),
        P(),
        P(),
    )
    return jax.shard_map(
        body, mesh=fine, in_specs=placed, out_specs=(P(None, COL), P(None, COL)), check_vma=False
    )
```

```python
import functools

import jax
import jax.numpy as jnp
from jax import lax
from jax.experimental import pallas as pl
from jax.experimental.pallas import tpu as pltpu
from jax.sharding import Mesh, PartitionSpec as P

B = 128
BLK = 128
CAP = 163
CHUNKS = (32, 32)
VEC = 64
SIZES = (16, 24, 24)
FIRST = tuple(sum(SIZES[:g]) for g in range(len(SIZES)))
ROW = ("x", "zl", "core")
COL = ("y", "zh")
ORDER = (
    "A0s", "B0s", "C0s", "A0a", "A0b", "B0a", "C0a", "A0c", "B0b", "C0b", "A0d", "B0c", "A0e",
    "C0c", "A0f", "B0d", "C0d", "B0e", "A0g", "C0e", "B0f", "C0f", "A1p", "B0g", "C0g", "B1p",
    "A1a", "C1p", "A1b", "B1a", "A1c", "C1a", "B1b", "A1d", "C1b", "B1c", "A1e", "C1c", "A1f",
    "B1d", "C1d", "B1e", "A1g", "C1e", "B1f", "C1f", "A1m", "B1g", "C1g", "B1m", "C1m",
)


def split(value):
    high = value.astype(jnp.bfloat16).astype(jnp.float32)
    return jnp.concatenate([high, value - high], axis=0).astype(jnp.bfloat16)


def ring_place(rel, core):
    one, three = 2 - core, 1 + core
    return jnp.where(rel == 0, 0, jnp.where(rel == 2, 3, jnp.where(rel == 1, one, three)))


def row_places(table):
    core, y, zh = (lax.axis_index(a) for a in ("core", "y", "zh"))
    for q in range(16):
        table[q] = ring_place(q // 4 ^ y, core) * 32 + ring_place(q % 4 ^ zh, core) * 8


def col_places(table, owners):
    x, zl, core = (lax.axis_index(a) for a in ROW)
    for r in range(16):
        side = r % 2
        spot = (side ^ core) * 8 + ring_place(r // 4 ^ x, 1 - side) * 2 + (r // 2 % 2 ^ zl)
        table[r] = spot * 8
        owners[spot] = r


def read_pattern(pattern, held, sems):
    copies = [pltpu.make_async_copy(p, h, sems.at[k]) for k, (p, h) in enumerate(zip(pattern, held))]
    for copy in copies:
        copy.start()
    return copies


def copy_tiles(tiles, held, sems, chunk):
    def one(c, size):
        span = pl.ds(c * chunk, size)
        return pltpu.make_async_copy(tiles.at[0, 0, span], held.at[span], sems.at[c])

    return one


def multiply(start, size, count, rows, cols, row_table, col_table, xs, held, acc):
    v = acc.shape[1]
    sums = []
    for u in range(size):
        col = cols[0, 0, start + u]
        if col_table is not None:
            col = col_table[col // 8] + col % 8
        p = lax.dot_general(
            xs[col], split(held[start + u]), (((1,), (1,)), ((), ())), preferred_element_type=jnp.float32
        )
        sums.append(p[:v, :B] + (p[v:, :B] + p[:v, B:]))
    for u in range(size):
        row = rows[0, 0, start + u]
        acc[jnp.where(start + u < count, row_table[row // 8] + row % 8, BLK)] += sums[u]


def over_chunks(count, chunk, work):
    whole = CAP // chunk

    def step(c, carry):
        work(c, chunk)
        return carry

    lax.fori_loop(0, jnp.minimum((count + chunk - 1) // chunk, whole), step, 0)
    if CAP % chunk:

        @pl.when(count > whole * chunk)
        def _():
            work(whole, CAP % chunk)


def send_out(acc, parts, outs, sems):
    copies = []
    for k, out in enumerate(outs):
        place = acc.at[pl.ds(k % 2 * 64, 64), pl.ds(sum(parts[: k // 2]), parts[k // 2])]
        copies.append(pltpu.make_async_copy(place, out, sems.at[k]))
    for copy in copies:
        copy.start()
    for copy in copies:
        copy.wait()


PATTERN = [pltpu.SMEM((1, 1, CAP), jnp.int32)] * 2
TABLES = [pltpu.SMEM((16,), jnp.int32)] * 3
TILES = [
    pltpu.VMEM((CAP, B, B), jnp.float32),
    pltpu.SemaphoreType.DMA((-(-CAP // min(CHUNKS)),)),
    pltpu.SemaphoreType.DMA((2,)),
]


def start_tiles(count, chunk, tile_copy):
    for c in range(-(-CAP // chunk)):

        @pl.when(c * chunk < count)
        def _():
            tile_copy(c, min(chunk, CAP - c * chunk)).start()


def first_kernel(live, rows_in, cols_in, tiles, panel_cur, panel_prev, *refs):
    n = 2 * len(SIZES)
    outs, (cur, prev), refs = refs[:n], refs[n : n + 2], refs[n + 2 :]
    (rows, cols), (row_table, _, _), (held, sems, p_sems) = refs[:2], refs[2:5], refs[5:8]
    xf, xp, xs, acc, x_sems, out_sems = refs[8:]
    mine = pl.multiple_of(((lax.axis_index("x") * 2 + lax.axis_index("zl")) * 2 + lax.axis_index("core")) * (8 * B), 8 * B)
    pattern = read_pattern((rows_in, cols_in), (rows, cols), p_sems)
    x_copies = []
    for k in range(4):
        span = pl.ds(k * 32 * B, 32 * B)
        x_copies.append(pltpu.make_async_copy(panel_cur.at[:, span], xf.at[:, span], x_sems.at[k]))
        x_copies[k].start()
    p_copy = pltpu.make_async_copy(panel_prev.at[:, pl.ds(mine, 8 * B)], xp, x_sems.at[4])
    count, chunk = live[0, 0], CHUNKS[0]
    tile_copy = copy_tiles(tiles, held, sems, chunk)
    start_tiles(count, chunk, tile_copy)
    p_copy.start()
    row_places(row_table)
    acc[...] = jnp.zeros_like(acc)
    for c in range(BLK):
        if c % 32 == 0:
            x_copies[c // 32].wait()
        xs[c] = split(xf[:, c * B : (c + 1) * B])
    for copy in pattern:
        copy.wait()
    for b in range(8):
        cur[b] = xf[:, pl.ds(mine + b * B, B)]

    def work(c, size):
        tile_copy(c, size).wait()
        multiply(c * chunk, size, count, rows, cols, row_table, None, xs, held, acc)

    over_chunks(count, chunk, work)
    p_copy.wait()
    for b in range(8):
        prev[b] = xp[:, b * B : (b + 1) * B]
    send_out(acc, SIZES, outs, out_sems)


def first_products(count, pattern, tiles, panel_cur, panel_prev):
    hbm = [pltpu.with_memory_space_constraint(a, pltpu.HBM) for a in (*pattern, tiles, panel_cur, panel_prev)]
    free = pl.BlockSpec(memory_space=pl.ANY)
    vmem = pl.BlockSpec(memory_space=pltpu.VMEM)
    n = 2 * len(SIZES)
    outs = pl.pallas_call(
        first_kernel,
        out_shape=[jax.ShapeDtypeStruct((64, v, B), jnp.float32) for v in SIZES for _ in range(2)]
        + [pltpu.VMEM((8, VEC, B), jnp.float32)] * 2,
        in_specs=[pl.BlockSpec(memory_space=pltpu.SMEM)] + [free] * 5,
        out_specs=[free] * n + [vmem] * 2,
        scratch_shapes=PATTERN + TABLES + TILES + [
            pltpu.VMEM((VEC, BLK * B), jnp.float32),
            pltpu.VMEM((VEC, 8 * B), jnp.float32),
            pltpu.VMEM((BLK, 2 * VEC, B), jnp.bfloat16),
            pltpu.VMEM((BLK + 1, VEC, B), jnp.float32),
            pltpu.SemaphoreType.DMA((5,)),
            pltpu.SemaphoreType.DMA((n,)),
        ],
        compiler_params=pltpu.CompilerParams(vmem_limit_bytes=26 << 20),
        cost_estimate=pl.CostEstimate(flops=1, bytes_accessed=1, transcendentals=0),
        name="first",
    )(count, *hbm)
    return [outs[i : i + 2] for i in range(0, n, 2)], outs[n], outs[n + 1]


def lay_out(x_own, x_other, owners, flat):
    for k in range(BLK // 8):
        start = pl.multiple_of(owners[k] * (8 * B), 8 * B)
        ref = x_own if k < 8 else x_other
        for b in range(8):
            flat[:, pl.ds(start + b * B, B)] = ref[k % 8 * 8 + b]


def second_kernel(first, live, rows_in, cols_in, tiles, x_own, x_other, *refs):
    keep, send, panel = refs[-16:-13]
    refs = refs[-13:]
    (rows, cols), (row_table, col_table, owners), (held, sems, p_sems) = refs[:2], refs[2:5], refs[5:8]
    xs, acc, flat, sem, out_sems = refs[8:]
    v = acc.shape[1]
    pattern = read_pattern((rows_in, cols_in), (rows, cols), p_sems)
    count, chunk = live[0, 0], CHUNKS[1]
    tile_copy = copy_tiles(tiles, held, sems, chunk)
    start_tiles(count, chunk, tile_copy)
    row_places(row_table)
    col_places(col_table, owners)
    lay_out(x_own, x_other, owners, flat)
    rows_copy = pltpu.make_async_copy(flat, panel.at[pl.ds(first, v)], sem)
    rows_copy.start()
    acc[...] = jnp.zeros_like(acc)
    for c in range(BLK):
        xs[c] = split((x_own if c < 64 else x_other)[c % 64])
    for copy in pattern:
        copy.wait()

    def work(c, size):
        tile_copy(c, size).wait()
        multiply(c * chunk, size, count, rows, cols, row_table, col_table, xs, held, acc)

    over_chunks(count, chunk, work)
    send_out(acc, (v,), (keep, send), out_sems)
    rows_copy.wait()


def second_products(count, pattern, tiles, x, panel, g):
    v = SIZES[g]
    free = pl.BlockSpec(memory_space=pl.ANY)
    vmem = pl.BlockSpec(memory_space=pltpu.VMEM)
    hbm = [pltpu.with_memory_space_constraint(a, pltpu.HBM) for a in (*pattern, tiles)]
    near = [pltpu.with_memory_space_constraint(a, pltpu.VMEM) for a in x]
    old = [] if panel is None else [panel]
    return pl.pallas_call(
        functools.partial(second_kernel, FIRST[g]),
        out_shape=[pltpu.VMEM((64, v, B), jnp.float32)] * 2 + [pltpu.HBM((VEC, BLK * B), jnp.float32)],
        in_specs=[pl.BlockSpec(memory_space=pltpu.SMEM)] + [free] * 3 + [vmem] * 2 + [free] * len(old),
        out_specs=[free] * 3,
        scratch_shapes=PATTERN + TABLES + TILES + [
            pltpu.VMEM((BLK, 2 * v, B), jnp.bfloat16),
            pltpu.VMEM((BLK + 1, v, B), jnp.float32),
            pltpu.VMEM((v, BLK * B), jnp.float32),
            pltpu.SemaphoreType.DMA,
            pltpu.SemaphoreType.DMA((2,)),
        ],
        input_output_aliases={6: 2} if old else {},
        compiler_params=pltpu.CompilerParams(vmem_limit_bytes=20 << 20),
        cost_estimate=pl.CostEstimate(flops=1, bytes_accessed=1, transcendentals=0),
        name="second",
    )(count, *hbm, *near, *old)


def assemble_kernel(first, v, x_own, x_other, *rest):
    out, table, owners, flat, sem = rest[-5:]
    col_places(table, owners)
    lay_out(x_own, x_other, owners, flat)
    copy = pltpu.make_async_copy(flat, out.at[pl.ds(first, v)], sem)
    copy.start()
    copy.wait()


def assemble(x, panel, g):
    v = SIZES[g]
    free = pl.BlockSpec(memory_space=pl.ANY)
    vmem = pl.BlockSpec(memory_space=pltpu.VMEM)
    held = [pltpu.with_memory_space_constraint(a, pltpu.VMEM) for a in x]
    old = [] if panel is None else [panel]
    return pl.pallas_call(
        functools.partial(assemble_kernel, FIRST[g], v),
        out_shape=pltpu.HBM((VEC, BLK * B), jnp.float32),
        in_specs=[vmem, vmem] + [free] * len(old),
        out_specs=free,
        scratch_shapes=TABLES[:2] + [pltpu.VMEM((v, BLK * B), jnp.float32), pltpu.SemaphoreType.DMA],
        input_output_aliases={2: 0} if old else {},
        compiler_params=pltpu.CompilerParams(vmem_limit_bytes=8 << 20),
        cost_estimate=pl.CostEstimate(flops=1, bytes_accessed=1, transcendentals=0),
        name="assemble",
    )(*held, *old)


def swap(value, axis):
    return lax.ppermute(value, axis, [(0, 1), (1, 0)])


def exchange(value, axis, turn):
    flip = {(0, 0): 1, (0, 1): 3, (1, 0): 3, (1, 1): 1}
    both, at = (("x", "core"), lambda c, i: i * 2 + c) if axis == "x" else (("core", axis), lambda c, i: c * 4 + i)
    pairs = [(at(c, i), at(c, i ^ flip[c, turn])) for c in range(2) for i in range(4)]
    return lax.ppermute(value, both, pairs)


def body(panel_prev, panel_cur, tiles, tile_rows, tile_cols, tile_count, center, halfwidth):
    pattern = (tile_rows, tile_cols)
    factor = 2.0 / halfwidth
    shares = {}
    panels = [None, None]

    first, cur, prev = first_products(tile_count, pattern, tiles, panel_cur, panel_prev)
    token = first[0][0]
    state = {(g, 0): [[keep], send] for g, (keep, send) in enumerate(first)}

    for event in ORDER:
        g, step, stage = ord(event[0]) - 65, int(event[1]), event[2]
        key = (g, step)
        if stage == "s":
            (state[key][1],), token = lax.optimization_barrier(((state[key][1],), token))
            continue
        if stage == "p":
            args, token = lax.optimization_barrier((state[g, 0], token))
            keep, token, panels[0] = second_products(tile_count, pattern, tiles, args, panels[0], g)
            state[key] = [[keep], token]
            continue
        if stage == "m":
            args, token = lax.optimization_barrier((state[key], token))
            panels[1] = token = assemble(args, panels[1], g)
            continue
        if stage in "abcd":
            kept, send = state[key]
            got = exchange(send, "y" if stage in "ab" else "zh", "abcd".index(stage) % 2)
        elif stage == "e":
            kept, got = [state[key]], swap(state[key], "zl")
        else:
            kept, got = [state[key]], exchange(state[key], "x", "fg".index(stage))
        (kept, got), token = lax.optimization_barrier(((kept, got), token))
        kept = [*kept, got]
        if stage in "abc":
            half = got.shape[0] // 2
            token = functools.reduce(jnp.add, [piece[half : 2 * half] for piece in kept])
            state[key] = [kept, token]
        elif stage == "d":
            mine = slice(FIRST[g], FIRST[g] + SIZES[g])
            now, before = (cur[:, mine], prev[:, mine]) if step == 0 else (shares[g], cur[:, mine])
            image = functools.reduce(jnp.add, [piece[: got.shape[0]] for piece in kept])
            state[key] = shares[g] = token = factor * (image - center * now) - before
        else:
            state[key] = token = jnp.concatenate(kept)
            if stage == "g":
                state[key] = [state[key], swap(state[key], "core")]
    return tuple(panels)


def solution(mesh):
    fine = Mesh(mesh.devices.reshape(4, 2, 2, 4, 4), ROW + COL)
    placed = (
        P(None, COL),
        P(None, COL),
        P(ROW, COL, None, None, None),
        P(ROW, COL, None),
        P(ROW, COL, None),
        P(ROW, COL),
        P(),
        P(),
    )
    return jax.shard_map(
        body, mesh=fine, in_specs=placed, out_specs=(P(None, COL), P(None, COL)), check_vma=False
    )
```
